128 devices in a mesh: rep: 16 (over x, z), pre: 8 (over y, core).
Axes of the slice: x: 4, y: 4, z: 4, core: 2. Of those that a mesh axis runs over, the one named last changes fastest.
Arguments:
- residual_in: bfloat16 [1024, 4608], P(('rep', 'pre')), may hold values from -6 to 6
- post_gain: float32 [4608], replicated, may hold values from 0.5 to 1.5
- queries: bfloat16 [1024, 4096], P('rep', 'pre'), may hold values from -6 to 6
- new_keys: bfloat16 [1024, 2048], P('rep', 'pre'), may hold values from -18 to 18
- new_values: bfloat16 [1024, 2048], P('rep', 'pre'), may hold values from -6 to 6
- prefix_keys: bfloat16 [131072, 2048], P('rep', 'pre'), may hold values from -200 to 200
- prefix_values: bfloat16 [131072, 2048], P('rep', 'pre'), may hold values from -6 to 6
- suffix_keys: bfloat16 [1024, 128, 2048], P('rep', None, 'pre'), may hold values from -18 to 18
- suffix_values: bfloat16 [1024, 128, 2048], P('rep', None, 'pre'), may hold values from -6 to 6
- suffix_len: int32 [1024], P('rep'), may hold values from 1 to 128, as said below
- slot_owner: int32 [1024], P('rep'), may hold values from 0 to 1023, as said below
- output_weight: bfloat16 [4096, 4608], P('pre'), may hold values from -2 to 2
Outputs:
- layer_out: bfloat16 [1024, 4608], P(('rep', 'pre'))
The draws below stay inside these ranges and needn't reach their ends.
Inputs may be any that keep to these rules, and one draw needn't show every extreme that they name: Slot c holds the cache of sequence slot_owner[c]; every sequence is held by exactly one slot. `suffix_len`: some slot holds exactly 128 live positions.
All inputs are finite; a program needn't handle non-finite values.
Results may differ from the reference program's by a relative error of at most 0.0041.
Values may be sent and summed in bfloat16 or wider, within the bound.
No kernel may reach another device: no remote copies, remote signals or barrier semaphores. Data moves between devices by JAX's collectives and lax.ppermute only.
A program may use at most 128 MiB of HBM per device.

```python
import math
import jax
import jax.numpy as jnp
from jax import lax

D = 4608
H = 32
KVH = 16
HD = 128
SEQ_ROW = 64
PRE_DEV = 8192
SUF = 128
NSEQ = 1024
PREFIX = 131072
N_REP = 16


def shared_queries(key):
    return jnp.clip(jax.random.normal(jax.random.fold_in(key, 101), (NSEQ, H * HD), jnp.float32), -6.0, 6.0)


def shared_owners(key):
    return jax.random.permutation(jax.random.fold_in(key, 102), NSEQ).astype(jnp.int32)


def paired_queries(base_rows):
    grouped = base_rows.reshape(base_rows.shape[0], KVH, 2, HD)
    return grouped[:, :, 0, :] + grouped[:, :, 1, :]


def draw_queries(key, part):
    base_rows = shared_queries(key)
    return base_rows.astype(jnp.bfloat16)


def draw_new_keys(key, part):
    base_rows = shared_queries(key)
    key = jax.random.fold_in(key, 2)
    jitter = jnp.clip(jax.random.normal(key, (NSEQ, KVH, HD), jnp.float32), -4.0, 4.0)
    values = 1.3 * paired_queries(base_rows) + 0.5 * jitter
    return jnp.clip(values, -18.0, 18.0).reshape(NSEQ, KVH * HD).astype(jnp.bfloat16)


def draw_suffix_keys(key, part):
    base_rows = shared_queries(key)
    owners = shared_owners(key)
    key = jax.random.fold_in(key, 3)
    key_one, key_two = jax.random.split(key)
    paired = paired_queries(base_rows)[owners]
    strength = jax.random.uniform(key_one, (NSEQ, SUF, KVH, 1), jnp.float32, 0.5, 1.1)
    jitter = jnp.clip(jax.random.normal(key_two, (NSEQ, SUF, KVH, HD), jnp.float32), -4.0, 4.0)
    values = strength * paired[:, None] + jitter
    return jnp.clip(values, -18.0, 18.0).reshape(NSEQ, SUF, KVH * HD).astype(jnp.bfloat16)


def draw_prefix_keys(key, part):
    key = jax.random.fold_in(key, 4)
    key_one = jax.random.fold_in(key, 0)
    ramp_scale = 2.7 + 0.5 * jnp.arange(PREFIX).astype(jnp.float32) / PREFIX
    values = jnp.clip(jax.random.normal(key_one, (PREFIX, KVH, HD), jnp.float32), -5.0, 5.0) * ramp_scale[:, None, None]
    return jnp.clip(values, -200.0, 200.0).reshape(PREFIX, KVH * HD).astype(jnp.bfloat16)


def draw_output_weight(key, part):
    key = jax.random.fold_in(key, 5)
    key_one = jax.random.fold_in(key, 0)
    key_three = jax.random.fold_in(key, 2)
    fan_scale = (H * HD) ** (-0.5)
    columns = jnp.exp(jax.random.uniform(key_one, (1, D), jnp.float32, 0.0, math.log(10.0)))
    entries = jnp.clip(jax.random.normal(key_three, (H * HD, D), jnp.float32), -5.0, 5.0)
    return jnp.clip(entries * fan_scale * columns, -2.0, 2.0).astype(jnp.bfloat16)


def draw_suffix_len(key, part):
    key = jax.random.fold_in(key, 6)
    key_one, key_two, key_three = jax.random.split(key, 3)
    groups = NSEQ // SEQ_ROW
    heavy_rep = jax.random.randint(key_one, (groups,), 0, 4) == 0
    forced = jax.random.randint(key_two, (), 0, NSEQ)
    heavy_rep = heavy_rep | (jnp.arange(groups) == forced // SEQ_ROW)
    factor = jnp.where(heavy_rep, 4, 1)
    base_len = jax.random.randint(key_three, (NSEQ,), 1, SUF // 3 + 1)
    slot_rep = jnp.arange(NSEQ) // SEQ_ROW
    lengths = jnp.minimum(base_len * factor[slot_rep], SUF)
    return jnp.where(jnp.arange(NSEQ) == forced, SUF, lengths).astype(jnp.int32)


def draw_slot_owner(key, part):
    owners = shared_owners(key)
    return owners


def steps_of(own_key, dims, pieces, least, high):
    gain = 1.0
    for dim, parts in pieces:
        steps = jax.random.uniform(jax.random.fold_in(jax.random.fold_in(own_key, 6), dim), (parts,), jnp.float32, least / len(pieces), high / len(pieces))
        gain = gain * jnp.repeat(jnp.exp(steps), dims[dim] // parts).reshape((-1,) + (1,) * (len(dims) - 1 - dim))
    return gain


def bell_draw(own_key, dims, deviation, reach, shards=(), kind=jnp.bfloat16):
    values = deviation * jax.random.normal(own_key, dims, jnp.float32)
    if shards:
        values = values * steps_of(own_key, dims, shards, -0.22, 0.18)
    return jnp.clip(values, -reach, reach).astype(kind)


def setup_inputs(seed: int = 0) -> dict:
    seeds = jax.random.split(jax.random.key(seed), 13)
    residual_in = bell_draw(seeds[0], (NSEQ, D), 1.0, 6.0, ((0, 128),))
    post_gain = jnp.clip(1.0 + 0.1 * jax.random.normal(seeds[1], (D,), jnp.float32), 0.5, 1.5)
    queries = draw_queries(jax.random.fold_in(seeds[12], 71), 0)
    new_keys = draw_new_keys(jax.random.fold_in(seeds[12], 71), 0)
    new_values = bell_draw(seeds[4], (NSEQ, KVH * HD), 1.0, 6.0, ((0, 16), (1, 8)))
    prefix_keys = draw_prefix_keys(jax.random.fold_in(seeds[12], 71), 0)
    prefix_values = bell_draw(seeds[6], (PREFIX, KVH * HD), 1.0, 6.0, ((0, 16), (1, 8)))
    suffix_keys = draw_suffix_keys(jax.random.fold_in(seeds[12], 71), 0)
    suffix_values = bell_draw(seeds[8], (NSEQ, SUF, KVH * HD), 1.0, 6.0, ((0, 16), (2, 8)))
    suffix_len = draw_suffix_len(jax.random.fold_in(seeds[12], 71), 0)
    slot_owner = draw_slot_owner(jax.random.fold_in(seeds[12], 71), 0)
    output_weight = draw_output_weight(jax.random.fold_in(seeds[12], 71), 0)
    return {"residual_in": residual_in, "post_gain": post_gain, "queries": queries, "new_keys": new_keys, "new_values": new_values, "prefix_keys": prefix_keys, "prefix_values": prefix_values, "suffix_keys": suffix_keys, "suffix_values": suffix_values, "suffix_len": suffix_len, "slot_owner": slot_owner, "output_weight": output_weight}


EPS = 1e-06

def rounded(values):
    return lax.optimization_barrier(values.astype(jnp.bfloat16)).astype(jnp.float32)

def block_partial(query_rows, key_rows, value_rows, score_scale):
    scores = jnp.einsum('sjd,td->sjt', query_rows, key_rows.astype(jnp.float32)) * score_scale
    block_top = lax.optimization_barrier(jnp.max(scores, axis=-1))
    exp_scores = jnp.exp(scores - block_top[..., None])
    totals = lax.optimization_barrier(jnp.sum(exp_scores, axis=-1))
    numerator = jnp.einsum('sjt,td->sjd', rounded(exp_scores), value_rows.astype(jnp.float32))
    return (block_top, totals, numerator)

def reference(residual_in, post_gain, queries, new_keys, new_values, prefix_keys, prefix_values, suffix_keys, suffix_values, suffix_len, slot_owner, output_weight):
    score_scale = (D // H) ** (-0.5)
    query_heads = queries.astype(jnp.float32).reshape(NSEQ, KVH, 2, HD)
    key_blocks = prefix_keys.reshape(N_REP, PRE_DEV, KVH, HD)
    value_blocks = prefix_values.reshape(N_REP, PRE_DEV, KVH, HD)

    def one_block(pair_blocks):
        key_block, value_block = pair_blocks

        def one_head(head_index):
            return block_partial(query_heads[:, head_index], key_block[:, head_index], value_block[:, head_index], score_scale)
        return lax.map(one_head, jnp.arange(KVH))
    block_top, block_total, block_numer = lax.map(one_block, (key_blocks, value_blocks))
    slot_queries = query_heads[slot_owner]
    own_keys = new_keys.astype(jnp.float32).reshape(NSEQ, KVH, HD)[slot_owner]
    own_values = new_values.astype(jnp.float32).reshape(NSEQ, KVH, HD)[slot_owner]
    cache_keys = suffix_keys.reshape(NSEQ, SUF, KVH, HD)
    cache_values = suffix_values.reshape(NSEQ, SUF, KVH, HD)
    live_mask = (jnp.arange(SUF)[None, :] < suffix_len[:, None])[:, None, :]

    def slot_head(head_index):
        query_rows = slot_queries[:, head_index]
        key_rows = cache_keys[:, :, head_index].astype(jnp.float32)
        value_rows = cache_values[:, :, head_index].astype(jnp.float32)
        scores = jnp.einsum('sjd,sud->sju', query_rows, key_rows) * score_scale
        own_score = jnp.einsum('sjd,sd->sj', query_rows, own_keys[:, head_index]) * score_scale
        slot_top = jnp.maximum(lax.optimization_barrier(jnp.max(jnp.where(live_mask, scores, -1e+30), axis=-1)), own_score)
        exp_scores = jnp.where(live_mask, jnp.exp(scores - slot_top[..., None]), 0.0)
        own_exp = jnp.exp(own_score - slot_top)
        totals = lax.optimization_barrier(jnp.sum(exp_scores, axis=-1)) + own_exp
        numerator = jnp.einsum('sju,sud->sjd', rounded(exp_scores), value_rows)
        numerator = numerator + rounded(own_exp)[..., None] * own_values[:, head_index][:, None, :]
        return (slot_top, totals, numerator)
    slot_top, slot_total, slot_numer = lax.map(slot_head, jnp.arange(KVH))
    slot_of = jnp.zeros((NSEQ,), jnp.int32).at[slot_owner].set(jnp.arange(NSEQ).astype(jnp.int32))
    slot_top = slot_top[:, slot_of]
    slot_total = slot_total[:, slot_of]
    slot_numer = slot_numer[:, slot_of]
    row_top = jnp.maximum(lax.optimization_barrier(jnp.max(block_top, axis=0)), slot_top)
    block_scale = jnp.exp(block_top - row_top[None])
    slot_scale = jnp.exp(slot_top - row_top)
    row_total = lax.optimization_barrier(jnp.sum(block_total * block_scale, axis=0)) + slot_total * slot_scale
    row_numer = lax.optimization_barrier(jnp.sum(block_numer * block_scale[..., None], axis=0)) + slot_numer * slot_scale[..., None]
    attention = (row_numer / row_total[..., None]).astype(jnp.bfloat16)
    attention = jnp.transpose(attention, (1, 0, 2, 3)).reshape(NSEQ, H * HD)
    mixed = jnp.dot(attention, output_weight, preferred_element_type=jnp.float32)
    mean_square = lax.optimization_barrier(jnp.mean(mixed * mixed, axis=-1, keepdims=True))
    return (residual_in.astype(jnp.float32) + post_gain * mixed * lax.rsqrt(mean_square + EPS)).astype(jnp.bfloat16)
```

```python
import functools
import math

import jax
import jax.numpy as jnp
from jax import lax
from jax.experimental import pallas as pl
from jax.experimental.pallas import tpu as pltpu
from jax.sharding import PartitionSpec as P

D = 4608
H = 32
HD = 128
EPS = 1e-06
NZ = 4
LOG2E = math.log2(math.e)
SCALE2 = (D // H) ** (-0.5) * LOG2E
LOW = -1e30
SAFE = 2.0**100
NT = (((1,), (1,)), ((), ()))
SAMPLE = 256
VMEM = 32 * 2**20
VMEM_ATT = 40 * 2**20
BF = jnp.bfloat16
F32 = jnp.float32


def pieces(x):
    hi = x.astype(BF)
    rest = x - hi.astype(F32)
    mid = rest.astype(BF)
    low = (rest - mid.astype(F32)).astype(BF)
    return hi, mid, low


def stat_tile(lse, rows):
    lane = lax.broadcasted_iota(jnp.int32, (rows, 128), 1)
    out = jnp.where(lane % 4 == 3, 1.0, 0.0)
    for h in range(4):
        for i, term in enumerate(pieces(lse[:, h * HD : (h + 1) * HD])):
            out = jnp.where(lane == 4 * h + i, term.astype(F32), out)
    return out.astype(BF)


def stat_spread(tile, flag=False):
    lane = lax.broadcasted_iota(jnp.int32, (128, 512), 0)
    head = lax.broadcasted_iota(jnp.int32, (128, 512), 1) // HD
    off = lane - 4 * head
    if flag:
        chosen = off == 3
    else:
        chosen = jnp.logical_and(off >= 0, off < 3)
    return jnp.dot(tile, jnp.where(chosen, 1.0, 0.0).astype(BF), preferred_element_type=F32)


def slot_rows(owner, count):
    bits = count.bit_length() - 1
    home = owner >> bits
    rep = lax.axis_index("rep")
    kx = (rep // NZ - (home >> 2)) & 3
    kz = (rep % NZ - (home & 3)) & 3
    return (kz << (bits + 2)) + (kx << bits) + (owner & (count - 1))


def find_slots(base, rows, owner_ref, pack_ref):
    where = slot_rows(owner_ref[...], pack_ref.shape[0])
    index = lax.broadcasted_iota(jnp.int32, (rows, where.shape[1]), 0) + base
    pick = jnp.where(index == where, 1.0, 0.0).astype(BF)
    found = jnp.dot(pick, pack_ref[...], preferred_element_type=F32)
    tile = found[:, 1024:].astype(BF)
    lse = jnp.where(stat_spread(tile, True) > 0.5, stat_spread(tile), LOW)
    return found[:, :512] + found[:, 512:1024], lse


def join(parts):
    both = functools.reduce(jnp.maximum, [x for _, x in parts])
    w = [jnp.exp2(x - both) for _, x in parts]
    mass = functools.reduce(jnp.add, w)
    o = functools.reduce(jnp.add, [v * x for (v, _), x in zip(parts, w)])
    return o / mass, both + jnp.log2(mass)


def opened(part):
    return part[:, :512].astype(F32), stat_spread(part[:, 512:])


def sampled(q_ref, k_ref, h):
    keys = k_ref[:SAMPLE, (h // 2) * HD : (h // 2 + 1) * HD]
    s = lax.dot_general(q_ref[:, h * HD : (h + 1) * HD], keys, NT, preferred_element_type=F32)
    return jnp.broadcast_to(jnp.max(s, axis=1, keepdims=True) * SCALE2, (q_ref.shape[0], 128))


def stage_kernel(q_ref, k_ref, o_ref):
    for h in range(4):
        o_ref[h] = sampled(q_ref, k_ref, h)


def stage(q, keys):
    rows = q.shape[0]
    return pl.pallas_call(
        stage_kernel,
        grid=(1,),
        in_specs=[
            pl.BlockSpec((rows, 512), lambda i: (0, 0)),
            pl.BlockSpec((SAMPLE, 256), lambda i: (0, 0)),
        ],
        out_specs=pl.BlockSpec((4, rows, 128), lambda i: (0, 0, 0)),
        out_shape=jax.ShapeDtypeStruct((4, rows, 128), F32),
        compiler_params=pltpu.CompilerParams(vmem_limit_bytes=VMEM),
        cost_estimate=pl.CostEstimate(flops=6 * 10**9, bytes_accessed=2**20, transcendentals=0),
        name="stage",
    )(q, keys)


def attend_body(q_ref, k_ref, v_ref, acc, top, first=None):
    rows = q_ref.shape[0]
    span = k_ref.shape[0]

    def lanes_of(n):
        return pl.ds(n * HD if isinstance(n, int) else pl.multiple_of(n * HD, HD), HD)

    def scores(h, keys):
        return lax.dot_general(q_ref[:, lanes_of(h)], keys, NT, preferred_element_type=F32)

    for h in range(4):
        top[h] = sampled(q_ref, k_ref, h) if first is None else first[h]

    def head_group(g, carry):
        values = jnp.concatenate([v_ref[:, lanes_of(g)], jnp.ones((span, 128), BF)], axis=1)
        keys = k_ref[:, lanes_of(g)]
        for h in (2 * g, 2 * g + 1):
            p = jnp.exp2(scores(h, keys) * SCALE2 - top[h][:, :1]).astype(BF)
            acc[h] = jnp.dot(p, values, preferred_element_type=F32)
        return carry

    lax.fori_loop(0, 2, head_group, 0)
    worst = jnp.zeros((rows, 128), F32)
    for h in range(4):
        worst = jnp.maximum(worst, jnp.where(acc[h][:, 128:] < SAFE, 0.0, 1.0))

    @pl.when(jnp.max(worst) > 0.0)
    def _():
        tile = math.gcd(span, 512)
        many = jnp.ones((tile, 128), BF)
        top[...] = jnp.full(top.shape, LOW, F32)
        acc[...] = jnp.zeros(acc.shape, F32)

        def tile_step(i, carry):
            h = i % 4
            part = pl.ds(pl.multiple_of((i // 4) * tile, tile), tile)
            values = jnp.concatenate([v_ref[part, lanes_of(h // 2)], many], axis=1)
            s = scores(h, k_ref[part, lanes_of(h // 2)]) * SCALE2
            old = top[h]
            new = jnp.maximum(old, jnp.max(s, axis=1, keepdims=True))
            p = jnp.exp2(s - new[:, :1]).astype(BF)
            fade = jnp.exp2(old - new)
            top[h] = new
            acc[h] = acc[h] * jnp.concatenate([fade, fade], axis=1) + jnp.dot(
                p, values, preferred_element_type=F32
            )
            return carry

        lax.fori_loop(0, 4 * (span // tile), tile_step, 0)

    totals = jnp.concatenate([acc[h][:, 128:] for h in range(4)], axis=1)
    o = jnp.concatenate([acc[h][:, :128] for h in range(4)], axis=1) / totals
    return o, jnp.concatenate([top[h] for h in range(4)], axis=1) + jnp.log2(totals)


def put(o_ref, o, lse):
    o_ref[:, :512] = o.astype(BF)
    o_ref[:, 512:] = stat_tile(lse, o_ref.shape[0])


def plain_kernel(q_ref, k_ref, v_ref, o_ref, acc, top):
    put(o_ref, *attend_body(q_ref, k_ref, v_ref, acc, top))


def staged_kernel(q_ref, k_ref, v_ref, first_ref, o_ref, acc, top):
    put(o_ref, *attend_body(q_ref, k_ref, v_ref, acc, top, first_ref))


def slotted_kernel(base, q_ref, k_ref, v_ref, owner_ref, pack_ref, o_ref, acc, top):
    part = attend_body(q_ref, k_ref, v_ref, acc, top)
    put(o_ref, *join([part, find_slots(base[0], o_ref.shape[0], owner_ref, pack_ref)]))


def own_part(q_ref, nk_ref, nv_ref):
    score, value = [], []
    for h in range(4):
        lanes = slice((h // 2) * HD, (h // 2 + 1) * HD)
        prod = q_ref[:, h * HD : (h + 1) * HD].astype(F32) * nk_ref[:, lanes].astype(F32)
        total = jnp.sum(prod, axis=1, keepdims=True) * SCALE2
        score.append(jnp.broadcast_to(total, (q_ref.shape[0], HD)))
        value.append(nv_ref[:, lanes].astype(F32))
    return jnp.concatenate(value, axis=1), jnp.concatenate(score, axis=1)


def attend(kernel, q, keys, values, extra=(), base=None):
    rows = q.shape[0]
    span = keys.shape[0]
    vmem = pl.BlockSpec(memory_space=pltpu.VMEM)
    specs = [vmem] * (3 + len(extra))
    first = []
    if base is not None:
        specs = [pl.BlockSpec(memory_space=pltpu.SMEM)] + specs
        first = [jnp.full((1,), base, jnp.int32)]
    return pl.pallas_call(
        kernel,
        in_specs=specs,
        out_shape=jax.ShapeDtypeStruct((rows, 640), BF),
        scratch_shapes=[
            pltpu.VMEM((4, rows, 256), F32),
            pltpu.VMEM((4, rows, 128), F32),
        ],
        compiler_params=pltpu.CompilerParams(vmem_limit_bytes=VMEM_ATT),
        cost_estimate=pl.CostEstimate(
            flops=rows * 4 * span * 128, bytes_accessed=2**20, transcendentals=0
        ),
        name="attend",
    )(*first, q, keys, values, *extra)


def column(row):
    n = row.shape[1]
    same = lax.broadcasted_iota(jnp.int32, (n, n), 0) == lax.broadcasted_iota(jnp.int32, (n, n), 1)
    return jnp.sum(jnp.where(same, row.astype(F32), 0.0), axis=1, keepdims=True).astype(jnp.int32)


def slot_kernel(offset, owner_ref, lens_ref, g0, g1, g2, g3, k_ref, v_ref, part_ref, o_ref, merged_ref):
    count, depth, _ = k_ref.shape
    cols = count * depth
    size = g0.shape[0]
    where = column(slot_rows(owner_ref[...], count))
    q = jnp.zeros((count, 512), F32)
    for n, ref in enumerate((g0, g1, g2, g3)):
        index = lax.broadcasted_iota(jnp.int32, (count, size), 1) + n * size
        pick = jnp.where(index == where, 1.0, 0.0).astype(BF)
        q += jnp.dot(pick, ref[...], preferred_element_type=F32)
    q = q.astype(BF)
    off = lax.broadcasted_iota(jnp.int32, (count, cols), 1)
    off = off - depth * lax.broadcasted_iota(jnp.int32, (count, cols), 0)
    live = jnp.logical_and(off >= 0, off < column(lens_ref[...]))
    mask = jnp.where(live, 0.0, LOW)
    ones = jnp.ones((cols, 128), BF)
    lse = []
    for g in range(2):
        lanes = slice(g * HD, (g + 1) * HD)
        keys = k_ref[:, :, lanes].reshape(cols, HD)
        values = jnp.concatenate([v_ref[:, :, lanes].reshape(cols, HD), ones], axis=1)
        qq = [q[:, h * HD : (h + 1) * HD] for h in (2 * g, 2 * g + 1)]
        s = lax.dot_general(
            jnp.concatenate(qq, axis=0), keys, NT, preferred_element_type=F32
        )
        s = s * SCALE2 + jnp.concatenate([mask, mask], axis=0)
        m = jnp.max(s, axis=1, keepdims=True)
        acc = jnp.dot(jnp.exp2(s - m).astype(BF), values, preferred_element_type=F32)
        total = acc[:, 128:]
        both = acc[:, :128] / total
        log = m + jnp.log2(total)
        for j in range(2):
            h = 2 * g + j
            o = both[j * count : (j + 1) * count]
            hi = o.astype(BF)
            o_ref[:, h * HD : (h + 1) * HD] = hi
            o_ref[:, 512 + h * HD : 512 + (h + 1) * HD] = (o - hi.astype(F32)).astype(BF)
            lse.append(log[j * count : (j + 1) * count])
    o_ref[:, 1024:] = stat_tile(jnp.concatenate(lse, axis=1), count)
    found = find_slots(offset * size, part_ref.shape[0], owner_ref, o_ref)
    put(merged_ref, *join([opened(part_ref[...]), found]))


def slots(offset, owner, lens, groups, keys, values, part):
    count, depth, _ = keys.shape
    return pl.pallas_call(
        functools.partial(slot_kernel, offset),
        out_shape=[
            jax.ShapeDtypeStruct((count, 1152), BF),
            jax.ShapeDtypeStruct(part.shape, BF),
        ],
        compiler_params=pltpu.CompilerParams(vmem_limit_bytes=VMEM),
        cost_estimate=pl.CostEstimate(
            flops=10**9, bytes_accessed=2**20, transcendentals=0
        ),
        name="slots",
    )(owner, lens, *groups, keys, values, part)


def merge_kernel(q_ref, nk_ref, nv_ref, mine, z1, z2, z3, owner_ref, pack_ref, *o_refs):
    count = q_ref.shape[0]
    for i, out in enumerate(o_refs):
        rows = slice(i * count, (i + 1) * count)
        parts = [opened(r[rows, :]) for r in (mine, z1, z2, z3)]
        if i == 0:
            parts.append(own_part(q_ref, nk_ref, nv_ref))
        put(out, *join(parts + [find_slots(i * count, count, owner_ref, pack_ref)]))


def merge(new, mine, z, owner, pack):
    count = new[0].shape[0]
    return pl.pallas_call(
        merge_kernel,
        out_shape=[jax.ShapeDtypeStruct((count, 640), BF)] * (mine.shape[0] // count),
        compiler_params=pltpu.CompilerParams(vmem_limit_bytes=VMEM),
        cost_estimate=pl.CostEstimate(flops=10**8, bytes_accessed=2**21, transcendentals=0),
        name="merge",
    )(*new, mine, *z, owner, pack)


def project_kernel(mine, x1, x2, x3, w_ref, keep_ref, send_ref, att):
    rows = mine.shape[0]
    att[...], _ = join([opened(r[...]) for r in (mine, x1, x2, x3)])
    pre = lax.axis_index("pre")
    y = pre // 2
    core = pre % 2
    blocks = []
    for c in (core, 1 - core):
        for k in range(4):
            p = 2 * lax.rem(y + k, 4) + c
            blocks.append(att[pl.ds(pl.multiple_of(p * 8, 8), 8), :])
    ordered = jnp.concatenate(blocks, axis=0).astype(BF)
    out = jnp.dot(ordered, w_ref[...], preferred_element_type=F32)
    keep_ref[...] = out[: rows // 2]
    send_ref[...] = out[rows // 2 :].astype(BF)


def project(parts, w):
    rows = parts[0].shape[0]
    depth, width = w.shape
    return pl.pallas_call(
        project_kernel,
        out_shape=[
            jax.ShapeDtypeStruct((rows // 2, width), F32),
            jax.ShapeDtypeStruct((rows // 2, width), BF),
        ],
        scratch_shapes=[pltpu.VMEM((rows, 512), F32)],
        compiler_params=pltpu.CompilerParams(vmem_limit_bytes=VMEM),
        cost_estimate=pl.CostEstimate(flops=10**9, bytes_accessed=depth * width * 2, transcendentals=0),
        name="project",
    )(*parts, w)


def pair_kernel(keep_ref, got_ref, own_ref, s1, s2, s3):
    total = keep_ref[...] + got_ref[...].astype(F32)
    own_ref[...] = total[:8]
    for k, out in enumerate((s1, s2, s3)):
        out[...] = total[8 * (k + 1) : 8 * (k + 2)].astype(BF)


def pair(keep, got):
    width = keep.shape[1]
    return pl.pallas_call(
        pair_kernel,
        out_shape=[jax.ShapeDtypeStruct((8, width), F32)] + [jax.ShapeDtypeStruct((8, width), BF)] * 3,
        compiler_params=pltpu.CompilerParams(vmem_limit_bytes=VMEM),
        cost_estimate=pl.CostEstimate(flops=10**6, bytes_accessed=2**20, transcendentals=0),
        name="pair",
    )(keep, got)


def finish_kernel(own, r1, r2, r3, res, gain, o_ref):
    mixed = own[...] + r1[...].astype(F32) + r2[...].astype(F32) + r3[...].astype(F32)
    square = jnp.mean(mixed * mixed, axis=1, keepdims=True)
    o_ref[...] = (res[...].astype(F32) + gain[...] * mixed * lax.rsqrt(square + EPS)).astype(BF)


def finish(own, got, res, gain):
    return pl.pallas_call(
        finish_kernel,
        out_shape=jax.ShapeDtypeStruct(res.shape, BF),
        compiler_params=pltpu.CompilerParams(vmem_limit_bytes=VMEM),
        cost_estimate=pl.CostEstimate(flops=10**6, bytes_accessed=2**19, transcendentals=0),
        name="finish",
    )(own, *got, res, gain)


def shift_x(a, k):
    return lax.ppermute(a, "rep", [(i, ((i // NZ + k) % 4) * NZ + i % NZ) for i in range(16)])


def shift_z(a, k):
    return lax.ppermute(a, "rep", [(i, (i // NZ) * NZ + (i % NZ + k) % NZ) for i in range(16)])


def shift_y(a, k):
    return lax.ppermute(a, "pre", [(i, ((i // 2 + k) % 4) * 2 + i % 2) for i in range(8)])


def swap_core(a):
    return lax.ppermute(a, "pre", [(i, i ^ 1) for i in range(8)])


def shards(
    residual_in,
    post_gain,
    queries,
    new_keys,
    new_values,
    prefix_keys,
    prefix_values,
    suffix_keys,
    suffix_values,
    suffix_len,
    slot_owner,
    output_weight,
):
    count = queries.shape[0]
    line = [queries] + [shift_x(queries, k) for k in (1, 2, 3)]
    owner = slot_owner[None, :]
    group0 = jnp.concatenate(line, axis=0)
    size = group0.shape[0]
    order = (1, 2, 3)
    rest = {k: shift_z(group0, k) for k in order}

    shifts = stage(group0, prefix_keys)
    shifts, rest[order[0]] = lax.optimization_barrier((shifts, rest[order[0]]))
    early = attend(plain_kernel, rest[order[0]], prefix_keys, prefix_values)
    groups = [group0, rest[1], rest[2], rest[3]]
    pack, part = slots(
        order[0], owner, suffix_len[None, :], groups, suffix_keys, suffix_values, early
    )
    back = [shift_z(part, -order[0])]
    for k in order[1:]:
        part = attend(
            slotted_kernel, rest[k], prefix_keys, prefix_values, [owner, pack], k * size
        )
        back.append(shift_z(part, -k))
    late = attend(staged_kernel, group0, prefix_keys, prefix_values, [shifts])
    mine, *give = merge([queries, new_keys, new_values], late, back, owner, pack)
    x = [shift_x(a, -k) for k, a in zip((1, 2, 3), give)]
    keep, send = project([mine, *x], output_weight)
    kept, *give = pair(keep, swap_core(send))
    got = [shift_y(a, k) for k, a in zip((1, 2, 3), give)]
    return finish(kept, got, residual_in, post_gain[None, :])


def solution(mesh):
    return jax.shard_map(
        shards,
        mesh=mesh,
        in_specs=(
            P(("rep", "pre"), None),
            P(),
            P("rep", "pre"),
            P("rep", "pre"),
            P("rep", "pre"),
            P("rep", "pre"),
            P("rep", "pre"),
            P("rep", None, "pre"),
            P("rep", None, "pre"),
            P("rep"),
            P("rep"),
            P("pre", None),
        ),
        out_specs=P(("rep", "pre"), None),
        check_vma=False,
    )
```

```python
import functools
import math

import jax
import jax.numpy as jnp
from jax import lax
from jax.experimental import pallas as pl
from jax.experimental.pallas import tpu as pltpu
from jax.sharding import PartitionSpec as P

D = 4608
H = 32
HD = 128
EPS = 1e-06
NZ = 4
LOG2E = math.log2(math.e)
SCALE2 = (D // H) ** (-0.5) * LOG2E
LOW = -1e30
SAFE = 2.0**100
NT = (((1,), (1,)), ((), ()))
SAMPLE = 256
VMEM = 32 * 2**20
VMEM_ATT = 40 * 2**20
BF = jnp.bfloat16
F32 = jnp.float32


def pieces(x):
    hi = x.astype(BF)
    rest = x - hi.astype(F32)
    mid = rest.astype(BF)
    low = (rest - mid.astype(F32)).astype(BF)
    return hi, mid, low


def stat_tile(lse, rows):
    lane = lax.broadcasted_iota(jnp.int32, (rows, 128), 1)
    out = jnp.where(lane % 4 == 3, 1.0, 0.0)
    for h in range(4):
        for i, term in enumerate(pieces(lse[:, h * HD : (h + 1) * HD])):
            out = jnp.where(lane == 4 * h + i, term.astype(F32), out)
    return out.astype(BF)


def stat_spread(tile, flag=False):
    lane = lax.broadcasted_iota(jnp.int32, (128, 512), 0)
    head = lax.broadcasted_iota(jnp.int32, (128, 512), 1) // HD
    off = lane - 4 * head
    if flag:
        chosen = off == 3
    else:
        chosen = jnp.logical_and(off >= 0, off < 3)
    return jnp.dot(tile, jnp.where(chosen, 1.0, 0.0).astype(BF), preferred_element_type=F32)


def slot_rows(owner, count):
    bits = count.bit_length() - 1
    home = owner >> bits
    rep = lax.axis_index("rep")
    kx = (rep // NZ - (home >> 2)) & 3
    kz = (rep % NZ - (home & 3)) & 3
    return (kz << (bits + 2)) + (kx << bits) + (owner & (count - 1))


def find_slots(base, rows, owner_ref, pack_ref):
    where = slot_rows(owner_ref[...], pack_ref.shape[0])
    index = lax.broadcasted_iota(jnp.int32, (rows, where.shape[1]), 0) + base
    pick = jnp.where(index == where, 1.0, 0.0).astype(BF)
    found = jnp.dot(pick, pack_ref[...], preferred_element_type=F32)
    tile = found[:, 1024:].astype(BF)
    lse = jnp.where(stat_spread(tile, True) > 0.5, stat_spread(tile), LOW)
    return found[:, :512] + found[:, 512:1024], lse


def join(parts):
    both = functools.reduce(jnp.maximum, [x for _, x in parts])
    w = [jnp.exp2(x - both) for _, x in parts]
    mass = functools.reduce(jnp.add, w)
    o = functools.reduce(jnp.add, [v * x for (v, _), x in zip(parts, w)])
    return o / mass, both + jnp.log2(mass)


def opened(part):
    return part[:, :512].astype(F32), stat_spread(part[:, 512:])


def sampled(q_ref, k_ref, h):
    keys = k_ref[:SAMPLE, (h // 2) * HD : (h // 2 + 1) * HD]
    s = lax.dot_general(q_ref[:, h * HD : (h + 1) * HD], keys, NT, preferred_element_type=F32)
    return jnp.broadcast_to(jnp.max(s, axis=1, keepdims=True) * SCALE2, (q_ref.shape[0], 128))


def stage_kernel(q_ref, k_ref, o_ref):
    for h in range(4):
        o_ref[h] = sampled(q_ref, k_ref, h)


def stage(q, keys):
    rows = q.shape[0]
    return pl.pallas_call(
        stage_kernel,
        grid=(1,),
        in_specs=[
            pl.BlockSpec((rows, 512), lambda i: (0, 0)),
            pl.BlockSpec((SAMPLE, 256), lambda i: (0, 0)),
        ],
        out_specs=pl.BlockSpec((4, rows, 128), lambda i: (0, 0, 0)),
        out_shape=jax.ShapeDtypeStruct((4, rows, 128), F32),
        compiler_params=pltpu.CompilerParams(vmem_limit_bytes=VMEM),
        cost_estimate=pl.CostEstimate(flops=6 * 10**9, bytes_accessed=2**20, transcendentals=0),
        name="stage",
    )(q, keys)


def attend_body(q_ref, k_ref, v_ref, acc, top, first=None, start=0):
    rows = acc.shape[1]
    span = k_ref.shape[0]
    mine = slice(start, start + rows)

    def lanes_of(n):
        return pl.ds(n * HD if isinstance(n, int) else pl.multiple_of(n * HD, HD), HD)

    def scores(heads, keys):
        q = [q_ref[mine, lanes_of(h)] for h in heads]
        q = jnp.concatenate(q, axis=0) if len(q) > 1 else q[0]
        return lax.dot_general(q, keys, NT, preferred_element_type=F32)

    for h in range(4):
        top[h] = sampled(q_ref, k_ref, h) if first is None else first[h, mine]

    def head_group(g, carry):
        values = jnp.concatenate([v_ref[:, lanes_of(g)], jnp.ones((span, 128), BF)], axis=1)
        keys = k_ref[:, lanes_of(g)]
        pair = [2 * g, 2 * g + 1]
        for heads in [pair] if rows < 128 else [pair[:1], pair[1:]]:
            shift = [top[h][:, :1] for h in heads]
            shift = jnp.concatenate(shift, axis=0) if len(shift) > 1 else shift[0]
            p = jnp.exp2(scores(heads, keys) * SCALE2 - shift).astype(BF)
            out = jnp.dot(p, values, preferred_element_type=F32)
            for n, h in enumerate(heads):
                acc[h] = out[n * rows : (n + 1) * rows]
        return carry

    lax.fori_loop(0, 2, head_group, 0)
    worst = jnp.zeros((rows, 128), F32)
    for h in range(4):
        worst = jnp.maximum(worst, jnp.where(acc[h][:, 128:] < SAFE, 0.0, 1.0))

    @pl.when(jnp.max(worst) > 0.0)
    def _():
        tile = math.gcd(span, 512)
        many = jnp.ones((tile, 128), BF)
        top[...] = jnp.full(top.shape, LOW, F32)
        acc[...] = jnp.zeros(acc.shape, F32)

        def tile_step(i, carry):
            h = i % 4
            part = pl.ds(pl.multiple_of((i // 4) * tile, tile), tile)
            values = jnp.concatenate([v_ref[part, lanes_of(h // 2)], many], axis=1)
            s = scores([h], k_ref[part, lanes_of(h // 2)]) * SCALE2
            old = top[h]
            new = jnp.maximum(old, jnp.max(s, axis=1, keepdims=True))
            p = jnp.exp2(s - new[:, :1]).astype(BF)
            fade = jnp.exp2(old - new)
            top[h] = new
            acc[h] = acc[h] * jnp.concatenate([fade, fade], axis=1) + jnp.dot(
                p, values, preferred_element_type=F32
            )
            return carry

        lax.fori_loop(0, 4 * (span // tile), tile_step, 0)

    totals = jnp.concatenate([acc[h][:, 128:] for h in range(4)], axis=1)
    o = jnp.concatenate([acc[h][:, :128] for h in range(4)], axis=1) / totals
    return o, jnp.concatenate([top[h] for h in range(4)], axis=1) + jnp.log2(totals)


def put(o_ref, o, lse):
    o_ref[:, :512] = o.astype(BF)
    o_ref[:, 512:] = stat_tile(lse, o_ref.shape[0])


def put_local(o_ref, o, lse):
    o_ref[:, :512] = o
    o_ref[:, 512:] = lse


def local(part):
    return part[:, :512], part[:, 512:]


def plain_kernel(q_ref, k_ref, v_ref, o_ref, acc, top):
    put_local(o_ref, *attend_body(q_ref, k_ref, v_ref, acc, top))


def staged_kernel(start, q_ref, k_ref, v_ref, first_ref, o_ref, acc, top):
    put_local(o_ref, *attend_body(q_ref, k_ref, v_ref, acc, top, first_ref, start))


def slotted_kernel(base, q_ref, k_ref, v_ref, owner_ref, pack_ref, o_ref, acc, top):
    part = attend_body(q_ref, k_ref, v_ref, acc, top)
    put(o_ref, *join([part, find_slots(base[0], o_ref.shape[0], owner_ref, pack_ref)]))


def own_part(q_ref, nk_ref, nv_ref):
    score, value = [], []
    for h in range(4):
        lanes = slice((h // 2) * HD, (h // 2 + 1) * HD)
        prod = q_ref[:, h * HD : (h + 1) * HD].astype(F32) * nk_ref[:, lanes].astype(F32)
        total = jnp.sum(prod, axis=1, keepdims=True) * SCALE2
        score.append(jnp.broadcast_to(total, (q_ref.shape[0], HD)))
        value.append(nv_ref[:, lanes].astype(F32))
    return jnp.concatenate(value, axis=1), jnp.concatenate(score, axis=1)


def attend(kernel, q, keys, values, extra=(), base=None, rows=None):
    rows = rows or q.shape[0]
    span = keys.shape[0]
    vmem = pl.BlockSpec(memory_space=pltpu.VMEM)
    specs = [vmem] * (3 + len(extra))
    first = []
    if base is not None:
        specs = [pl.BlockSpec(memory_space=pltpu.SMEM)] + specs
        first = [jnp.full((1,), base, jnp.int32)]
    return pl.pallas_call(
        kernel,
        in_specs=specs,
        out_shape=jax.ShapeDtypeStruct(
            *(((rows, 1024), F32) if base is None else ((rows, 640), BF))
        ),
        scratch_shapes=[
            pltpu.VMEM((4, rows, 256), F32),
            pltpu.VMEM((4, rows, 128), F32),
        ],
        compiler_params=pltpu.CompilerParams(vmem_limit_bytes=VMEM_ATT),
        cost_estimate=pl.CostEstimate(
            flops=rows * 4 * span * 128, bytes_accessed=2**20, transcendentals=0
        ),
        name="attend",
    )(*first, q, keys, values, *extra)


def column(row):
    n = row.shape[1]
    same = lax.broadcasted_iota(jnp.int32, (n, n), 0) == lax.broadcasted_iota(jnp.int32, (n, n), 1)
    return jnp.sum(jnp.where(same, row.astype(F32), 0.0), axis=1, keepdims=True).astype(jnp.int32)


def slot_kernel(offset, owner_ref, lens_ref, g0, g1, g2, g3, k_ref, v_ref, part_ref, o_ref, merged_ref):
    count, depth, _ = k_ref.shape
    cols = count * depth
    size = g0.shape[0]
    where = column(slot_rows(owner_ref[...], count))
    q = jnp.zeros((count, 512), F32)
    for n, ref in enumerate((g0, g1, g2, g3)):
        index = lax.broadcasted_iota(jnp.int32, (count, size), 1) + n * size
        pick = jnp.where(index == where, 1.0, 0.0).astype(BF)
        q += jnp.dot(pick, ref[...], preferred_element_type=F32)
    q = q.astype(BF)
    off = lax.broadcasted_iota(jnp.int32, (count, cols), 1)
    off = off - depth * lax.broadcasted_iota(jnp.int32, (count, cols), 0)
    live = jnp.logical_and(off >= 0, off < column(lens_ref[...]))
    mask = jnp.where(live, 0.0, LOW)
    ones = jnp.ones((cols, 128), BF)
    lse = []
    for g in range(2):
        lanes = slice(g * HD, (g + 1) * HD)
        keys = k_ref[:, :, lanes].reshape(cols, HD)
        values = jnp.concatenate([v_ref[:, :, lanes].reshape(cols, HD), ones], axis=1)
        qq = [q[:, h * HD : (h + 1) * HD] for h in (2 * g, 2 * g + 1)]
        s = lax.dot_general(
            jnp.concatenate(qq, axis=0), keys, NT, preferred_element_type=F32
        )
        s = s * SCALE2 + jnp.concatenate([mask, mask], axis=0)
        m = jnp.max(s, axis=1, keepdims=True)
        acc = jnp.dot(jnp.exp2(s - m).astype(BF), values, preferred_element_type=F32)
        total = acc[:, 128:]
        both = acc[:, :128] / total
        log = m + jnp.log2(total)
        for j in range(2):
            h = 2 * g + j
            o = both[j * count : (j + 1) * count]
            hi = o.astype(BF)
            o_ref[:, h * HD : (h + 1) * HD] = hi
            o_ref[:, 512 + h * HD : 512 + (h + 1) * HD] = (o - hi.astype(F32)).astype(BF)
            lse.append(log[j * count : (j + 1) * count])
    o_ref[:, 1024:] = stat_tile(jnp.concatenate(lse, axis=1), count)
    found = find_slots(offset * size, part_ref.shape[0], owner_ref, o_ref)
    put(merged_ref, *join([local(part_ref), found]))


def slots(offset, owner, lens, groups, keys, values, part):
    count, depth, _ = keys.shape
    return pl.pallas_call(
        functools.partial(slot_kernel, offset),
        out_shape=[
            jax.ShapeDtypeStruct((count, 1152), BF),
            jax.ShapeDtypeStruct((part.shape[0], 640), BF),
        ],
        compiler_params=pltpu.CompilerParams(vmem_limit_bytes=VMEM),
        cost_estimate=pl.CostEstimate(
            flops=10**9, bytes_accessed=2**20, transcendentals=0
        ),
        name="slots",
    )(owner, lens, *groups, keys, values, part)


def merge_kernel(z1, z2, z3, owner_ref, pack_ref, late, *o_refs):
    count = o_refs[0].shape[0]
    for i, out in enumerate(o_refs):
        rows = slice((i + 1) * count, (i + 2) * count)
        parts = [opened(r[rows, :]) for r in (z1, z2, z3)]
        parts.append(local(late[i * count : (i + 1) * count, :]))
        put(out, *join(parts + [find_slots((i + 1) * count, count, owner_ref, pack_ref)]))


def home_kernel(z1, z2, z3, owner_ref, pack_ref, late, q_ref, nk_ref, nv_ref, out):
    count = out.shape[0]
    parts = [opened(r[:count, :]) for r in (z1, z2, z3)]
    parts += [local(late), own_part(q_ref, nk_ref, nv_ref)]
    put_local(out, *join(parts + [find_slots(0, count, owner_ref, pack_ref)]))


def merge(kernel, shapes, *args):
    return pl.pallas_call(
        kernel,
        out_shape=shapes,
        compiler_params=pltpu.CompilerParams(vmem_limit_bytes=VMEM),
        cost_estimate=pl.CostEstimate(flops=10**8, bytes_accessed=2**21, transcendentals=0),
        name="merge",
    )(*args)


def project_kernel(mine, x1, x2, x3, w_ref, keep_ref, send_ref, att):
    rows = mine.shape[0]
    att[...], _ = join([local(mine)] + [opened(r[...]) for r in (x1, x2, x3)])
    pre = lax.axis_index("pre")
    y = pre // 2
    core = pre % 2
    blocks = []
    for c in (core, 1 - core):
        for k in range(4):
            p = 2 * lax.rem(y + k, 4) + c
            blocks.append(att[pl.ds(pl.multiple_of(p * 8, 8), 8), :])
    ordered = jnp.concatenate(blocks, axis=0).astype(BF)
    out = jnp.dot(ordered, w_ref[...], preferred_element_type=F32)
    keep_ref[...] = out[: rows // 2]
    send_ref[...] = out[rows // 2 :].astype(BF)


def project(parts, w):
    rows = parts[0].shape[0]
    depth, width = w.shape
    return pl.pallas_call(
        project_kernel,
        out_shape=[
            jax.ShapeDtypeStruct((rows // 2, width), F32),
            jax.ShapeDtypeStruct((rows // 2, width), BF),
        ],
        scratch_shapes=[pltpu.VMEM((rows, 512), F32)],
        compiler_params=pltpu.CompilerParams(vmem_limit_bytes=VMEM),
        cost_estimate=pl.CostEstimate(flops=10**9, bytes_accessed=depth * width * 2, transcendentals=0),
        name="project",
    )(*parts, w)


def pair_kernel(keep_ref, got_ref, own_ref, s1, s2, s3):
    total = keep_ref[...] + got_ref[...].astype(F32)
    own_ref[...] = total[:8]
    for k, out in enumerate((s1, s2, s3)):
        out[...] = total[8 * (k + 1) : 8 * (k + 2)].astype(BF)


def pair(keep, got):
    width = keep.shape[1]
    return pl.pallas_call(
        pair_kernel,
        out_shape=[jax.ShapeDtypeStruct((8, width), F32)] + [jax.ShapeDtypeStruct((8, width), BF)] * 3,
        compiler_params=pltpu.CompilerParams(vmem_limit_bytes=VMEM),
        cost_estimate=pl.CostEstimate(flops=10**6, bytes_accessed=2**20, transcendentals=0),
        name="pair",
    )(keep, got)


def finish_kernel(own, r1, r2, r3, res, gain, o_ref):
    mixed = own[...] + r1[...].astype(F32) + r2[...].astype(F32) + r3[...].astype(F32)
    square = jnp.mean(mixed * mixed, axis=1, keepdims=True)
    o_ref[...] = (res[...].astype(F32) + gain[...] * mixed * lax.rsqrt(square + EPS)).astype(BF)


def finish(own, got, res, gain):
    return pl.pallas_call(
        finish_kernel,
        out_shape=jax.ShapeDtypeStruct(res.shape, BF),
        compiler_params=pltpu.CompilerParams(vmem_limit_bytes=VMEM),
        cost_estimate=pl.CostEstimate(flops=10**6, bytes_accessed=2**19, transcendentals=0),
        name="finish",
    )(own, *got, res, gain)


def shift_x(a, k):
    return lax.ppermute(a, "rep", [(i, ((i // NZ + k) % 4) * NZ + i % NZ) for i in range(16)])


def shift_z(a, k):
    return lax.ppermute(a, "rep", [(i, (i // NZ) * NZ + (i % NZ + k) % NZ) for i in range(16)])


def shift_y(a, k):
    return lax.ppermute(a, "pre", [(i, ((i // 2 + k) % 4) * 2 + i % 2) for i in range(8)])


def swap_core(a):
    return lax.ppermute(a, "pre", [(i, i ^ 1) for i in range(8)])


def shards(
    residual_in,
    post_gain,
    queries,
    new_keys,
    new_values,
    prefix_keys,
    prefix_values,
    suffix_keys,
    suffix_values,
    suffix_len,
    slot_owner,
    output_weight,
):
    count = queries.shape[0]
    line = [queries] + [shift_x(queries, k) for k in (1, 2, 3)]
    owner = slot_owner[None, :]
    group0 = jnp.concatenate(line, axis=0)
    size = group0.shape[0]
    order = (1, 2, 3)
    rest = {k: shift_z(group0, k) for k in order}

    shifts = stage(group0, prefix_keys)
    shifts, rest[order[0]] = lax.optimization_barrier((shifts, rest[order[0]]))
    early = attend(plain_kernel, rest[order[0]], prefix_keys, prefix_values)
    groups = [group0, rest[1], rest[2], rest[3]]
    pack, part = slots(
        order[0], owner, suffix_len[None, :], groups, suffix_keys, suffix_values, early
    )
    back = [shift_z(part, -order[0])]
    for k in order[1:]:
        done = back[:-1]
        rest[k], part, *done = lax.optimization_barrier((rest[k], part, *done))
        back = done + back[-1:]
        part = attend(
            slotted_kernel, rest[k], prefix_keys, prefix_values, [owner, pack], k * size
        )
        back.append(shift_z(part, -k))
    group0, *done = lax.optimization_barrier((group0, *back[:-1]))
    back = done + back[-1:]
    wide = size - count
    late = attend(
        functools.partial(staged_kernel, count), group0, prefix_keys, prefix_values, [shifts], rows=wide
    )
    z = [*back, owner, pack]
    give = merge(merge_kernel, [jax.ShapeDtypeStruct((count, 640), BF)] * 3, *z, late)
    group0, *give = lax.optimization_barrier((group0, *give))
    x = [shift_x(a, -k) for k, a in zip((1, 2, 3), give)]
    near = attend(
        functools.partial(staged_kernel, 0), group0, prefix_keys, prefix_values, [shifts], rows=count
    )
    mine = merge(
        home_kernel,
        jax.ShapeDtypeStruct((count, 1024), F32),
        *z,
        near,
        queries,
        new_keys,
        new_values,
    )
    keep, send = project([mine, *x], output_weight)
    kept, *give = pair(keep, swap_core(send))
    got = [shift_y(a, k) for k, a in zip((1, 2, 3), give)]
    return finish(kept, got, residual_in, post_gain[None, :])


def solution(mesh):
    return jax.shard_map(
        shards,
        mesh=mesh,
        in_specs=(
            P(("rep", "pre"), None),
            P(),
            P("rep", "pre"),
            P("rep", "pre"),
            P("rep", "pre"),
            P("rep", "pre"),
            P("rep", "pre"),
            P("rep", None, "pre"),
            P("rep", None, "pre"),
            P("rep"),
            P("rep"),
            P("pre", None),
        ),
        out_specs=P(("rep", "pre"), None),
        check_vma=False,
    )
```

```python
import functools
import math

import jax
import jax.numpy as jnp
from jax import lax
from jax.experimental import pallas as pl
from jax.experimental.pallas import tpu as pltpu
from jax.sharding import PartitionSpec as P

D = 4608
H = 32
HD = 128
EPS = 1e-06
NZ = 4
LOG2E = math.log2(math.e)
SCALE2 = (D // H) ** (-0.5) * LOG2E
LOW = -1e30
SAFE = 2.0**100
NT = (((1,), (1,)), ((), ()))
SAMPLE = 256
VMEM = 32 * 2**20
VMEM_ATT = 40 * 2**20
BF = jnp.bfloat16
F32 = jnp.float32


def pieces(x):
    hi = x.astype(BF)
    rest = x - hi.astype(F32)
    mid = rest.astype(BF)
    low = (rest - mid.astype(F32)).astype(BF)
    return hi, mid, low


def stat_tile(lse, rows):
    lane = lax.broadcasted_iota(jnp.int32, (rows, 128), 1)
    out = jnp.where(lane % 4 == 3, 1.0, 0.0)
    for h in range(4):
        for i, term in enumerate(pieces(lse[:, h * HD : (h + 1) * HD])):
            out = jnp.where(lane == 4 * h + i, term.astype(F32), out)
    return out.astype(BF)


def stat_spread(tile, flag=False):
    lane = lax.broadcasted_iota(jnp.int32, (128, 512), 0)
    head = lax.broadcasted_iota(jnp.int32, (128, 512), 1) // HD
    off = lane - 4 * head
    if flag:
        chosen = off == 3
    else:
        chosen = jnp.logical_and(off >= 0, off < 3)
    return jnp.dot(tile, jnp.where(chosen, 1.0, 0.0).astype(BF), preferred_element_type=F32)


def slot_rows(owner, count):
    bits = count.bit_length() - 1
    home = owner >> bits
    rep = lax.axis_index("rep")
    kx = (rep // NZ - (home >> 2)) & 3
    kz = (rep % NZ - (home & 3)) & 3
    return (kz << (bits + 2)) + (kx << bits) + (owner & (count - 1))


def find_slots(base, rows, owner_ref, pack_ref):
    where = slot_rows(owner_ref[...], pack_ref.shape[0])
    index = lax.broadcasted_iota(jnp.int32, (rows, where.shape[1]), 0) + base
    pick = jnp.where(index == where, 1.0, 0.0).astype(BF)
    found = jnp.dot(pick, pack_ref[...], preferred_element_type=F32)
    tile = found[:, 1024:].astype(BF)
    lse = jnp.where(stat_spread(tile, True) > 0.5, stat_spread(tile), LOW)
    return found[:, :512] + found[:, 512:1024], lse


def join(parts):
    both = functools.reduce(jnp.maximum, [x for _, x in parts])
    w = [jnp.exp2(x - both) for _, x in parts]
    mass = functools.reduce(jnp.add, w)
    o = functools.reduce(jnp.add, [v * x for (v, _), x in zip(parts, w)])
    return o / mass, both + jnp.log2(mass)


def opened(part):
    return part[:, :512].astype(F32), stat_spread(part[:, 512:])


def sampled(q_ref, k_ref, h):
    keys = k_ref[:SAMPLE, (h // 2) * HD : (h // 2 + 1) * HD]
    s = lax.dot_general(q_ref[:, h * HD : (h + 1) * HD], keys, NT, preferred_element_type=F32)
    return jnp.broadcast_to(jnp.max(s, axis=1, keepdims=True) * SCALE2, (q_ref.shape[0], 128))


def stage_kernel(q_ref, k_ref, o_ref):
    for h in range(4):
        o_ref[h] = sampled(q_ref, k_ref, h)


def stage(q, keys):
    rows = q.shape[0]
    return pl.pallas_call(
        stage_kernel,
        grid=(1,),
        in_specs=[
            pl.BlockSpec((rows, 512), lambda i: (0, 0)),
            pl.BlockSpec((SAMPLE, 256), lambda i: (0, 0)),
        ],
        out_specs=pl.BlockSpec((4, rows, 128), lambda i: (0, 0, 0)),
        out_shape=jax.ShapeDtypeStruct((4, rows, 128), F32),
        compiler_params=pltpu.CompilerParams(vmem_limit_bytes=VMEM),
        cost_estimate=pl.CostEstimate(flops=6 * 10**9, bytes_accessed=2**20, transcendentals=0),
        name="stage",
    )(q, keys)


def attend_body(q_ref, k_ref, v_ref, acc, top, first=None, start=0):
    rows = acc.shape[1]
    span = k_ref.shape[0]
    mine = slice(start, start + rows)

    def lanes_of(n):
        return pl.ds(n * HD if isinstance(n, int) else pl.multiple_of(n * HD, HD), HD)

    def scores(heads, keys):
        q = [q_ref[mine, lanes_of(h)] for h in heads]
        q = jnp.concatenate(q, axis=0) if len(q) > 1 else q[0]
        return lax.dot_general(q, keys, NT, preferred_element_type=F32)

    for h in range(4):
        top[h] = sampled(q_ref, k_ref, h) if first is None else first[h, mine]

    def head_group(g, carry):
        values = jnp.concatenate([v_ref[:, lanes_of(g)], jnp.ones((span, 128), BF)], axis=1)
        keys = k_ref[:, lanes_of(g)]
        pair = [2 * g, 2 * g + 1]
        for heads in [pair] if rows < 128 else [pair[:1], pair[1:]]:
            shift = [top[h][:, :1] for h in heads]
            shift = jnp.concatenate(shift, axis=0) if len(shift) > 1 else shift[0]
            p = jnp.exp2(scores(heads, keys) * SCALE2 - shift).astype(BF)
            out = jnp.dot(p, values, preferred_element_type=F32)
            for n, h in enumerate(heads):
                acc[h] = out[n * rows : (n + 1) * rows]
        return carry

    lax.fori_loop(0, 2, head_group, 0)
    worst = jnp.zeros((rows, 128), F32)
    for h in range(4):
        worst = jnp.maximum(worst, jnp.where(acc[h][:, 128:] < SAFE, 0.0, 1.0))

    @pl.when(jnp.max(worst) > 0.0)
    def _():
        tile = math.gcd(span, 512)
        many = jnp.ones((tile, 128), BF)
        top[...] = jnp.full(top.shape, LOW, F32)
        acc[...] = jnp.zeros(acc.shape, F32)

        def tile_step(i, carry):
            h = i % 4
            part = pl.ds(pl.multiple_of((i // 4) * tile, tile), tile)
            values = jnp.concatenate([v_ref[part, lanes_of(h // 2)], many], axis=1)
            s = scores([h], k_ref[part, lanes_of(h // 2)]) * SCALE2
            old = top[h]
            new = jnp.maximum(old, jnp.max(s, axis=1, keepdims=True))
            p = jnp.exp2(s - new[:, :1]).astype(BF)
            fade = jnp.exp2(old - new)
            top[h] = new
            acc[h] = acc[h] * jnp.concatenate([fade, fade], axis=1) + jnp.dot(
                p, values, preferred_element_type=F32
            )
            return carry

        lax.fori_loop(0, 4 * (span // tile), tile_step, 0)

    totals = jnp.concatenate([acc[h][:, 128:] for h in range(4)], axis=1)
    o = jnp.concatenate([acc[h][:, :128] for h in range(4)], axis=1) / totals
    return o, jnp.concatenate([top[h] for h in range(4)], axis=1) + jnp.log2(totals)


def put(o_ref, o, lse):
    o_ref[:, :512] = o.astype(BF)
    o_ref[:, 512:] = stat_tile(lse, o_ref.shape[0])


def put_local(o_ref, o, lse):
    o_ref[:, :512] = o
    o_ref[:, 512:] = lse


def local(part):
    return part[:, :512], part[:, 512:]


def plain_kernel(q_ref, k_ref, v_ref, o_ref, acc, top):
    put_local(o_ref, *attend_body(q_ref, k_ref, v_ref, acc, top))


def staged_kernel(start, q_ref, k_ref, v_ref, first_ref, o_ref, acc, top):
    put_local(o_ref, *attend_body(q_ref, k_ref, v_ref, acc, top, first_ref, start))


def slotted_kernel(base, q_ref, k_ref, v_ref, owner_ref, pack_ref, o_ref, acc, top):
    part = attend_body(q_ref, k_ref, v_ref, acc, top)
    put(o_ref, *join([part, find_slots(base[0], o_ref.shape[0], owner_ref, pack_ref)]))


def own_part(q_ref, nk_ref, nv_ref):
    score, value = [], []
    for h in range(4):
        lanes = slice((h // 2) * HD, (h // 2 + 1) * HD)
        prod = q_ref[:, h * HD : (h + 1) * HD].astype(F32) * nk_ref[:, lanes].astype(F32)
        total = jnp.sum(prod, axis=1, keepdims=True) * SCALE2
        score.append(jnp.broadcast_to(total, (q_ref.shape[0], HD)))
        value.append(nv_ref[:, lanes].astype(F32))
    return jnp.concatenate(value, axis=1), jnp.concatenate(score, axis=1)


def attend(kernel, q, keys, values, extra=(), base=None, rows=None):
    rows = rows or q.shape[0]
    span = keys.shape[0]
    vmem = pl.BlockSpec(memory_space=pltpu.VMEM)
    specs = [vmem] * (3 + len(extra))
    first = []
    if base is not None:
        specs = [pl.BlockSpec(memory_space=pltpu.SMEM)] + specs
        first = [jnp.full((1,), base, jnp.int32)]
    return pl.pallas_call(
        kernel,
        in_specs=specs,
        out_shape=jax.ShapeDtypeStruct(
            *(((rows, 1024), F32) if base is None else ((rows, 640), BF))
        ),
        scratch_shapes=[
            pltpu.VMEM((4, rows, 256), F32),
            pltpu.VMEM((4, rows, 128), F32),
        ],
        compiler_params=pltpu.CompilerParams(vmem_limit_bytes=VMEM_ATT),
        cost_estimate=pl.CostEstimate(
            flops=rows * 4 * span * 128, bytes_accessed=2**20, transcendentals=0
        ),
        name="attend",
    )(*first, q, keys, values, *extra)


def column(row):
    n = row.shape[1]
    same = lax.broadcasted_iota(jnp.int32, (n, n), 0) == lax.broadcasted_iota(jnp.int32, (n, n), 1)
    return jnp.sum(jnp.where(same, row.astype(F32), 0.0), axis=1, keepdims=True).astype(jnp.int32)


def slot_kernel(offset, owner_ref, lens_ref, g0, g1, g2, g3, k_ref, v_ref, part_ref, o_ref, merged_ref):
    count, depth, _ = k_ref.shape
    cols = count * depth
    size = g0.shape[0]
    where = column(slot_rows(owner_ref[...], count))
    q = jnp.zeros((count, 512), F32)
    for n, ref in enumerate((g0, g1, g2, g3)):
        index = lax.broadcasted_iota(jnp.int32, (count, size), 1) + n * size
        pick = jnp.where(index == where, 1.0, 0.0).astype(BF)
        q += jnp.dot(pick, ref[...], preferred_element_type=F32)
    q = q.astype(BF)
    off = lax.broadcasted_iota(jnp.int32, (count, cols), 1)
    off = off - depth * lax.broadcasted_iota(jnp.int32, (count, cols), 0)
    live = jnp.logical_and(off >= 0, off < column(lens_ref[...]))
    mask = jnp.where(live, 0.0, LOW)
    ones = jnp.ones((cols, 128), BF)
    lse = []
    for g in range(2):
        lanes = slice(g * HD, (g + 1) * HD)
        keys = k_ref[:, :, lanes].reshape(cols, HD)
        values = jnp.concatenate([v_ref[:, :, lanes].reshape(cols, HD), ones], axis=1)
        qq = [q[:, h * HD : (h + 1) * HD] for h in (2 * g, 2 * g + 1)]
        s = lax.dot_general(
            jnp.concatenate(qq, axis=0), keys, NT, preferred_element_type=F32
        )
        s = s * SCALE2 + jnp.concatenate([mask, mask], axis=0)
        m = jnp.max(s, axis=1, keepdims=True)
        acc = jnp.dot(jnp.exp2(s - m).astype(BF), values, preferred_element_type=F32)
        total = acc[:, 128:]
        both = acc[:, :128] / total
        log = m + jnp.log2(total)
        for j in range(2):
            h = 2 * g + j
            o = both[j * count : (j + 1) * count]
            hi = o.astype(BF)
            o_ref[:, h * HD : (h + 1) * HD] = hi
            o_ref[:, 512 + h * HD : 512 + (h + 1) * HD] = (o - hi.astype(F32)).astype(BF)
            lse.append(log[j * count : (j + 1) * count])
    o_ref[:, 1024:] = stat_tile(jnp.concatenate(lse, axis=1), count)
    found = find_slots(offset * size, part_ref.shape[0], owner_ref, o_ref)
    put(merged_ref, *join([local(part_ref), found]))


def slots(offset, owner, lens, groups, keys, values, part):
    count, depth, _ = keys.shape
    return pl.pallas_call(
        functools.partial(slot_kernel, offset),
        out_shape=[
            jax.ShapeDtypeStruct((count, 1152), BF),
            jax.ShapeDtypeStruct((part.shape[0], 640), BF),
        ],
        compiler_params=pltpu.CompilerParams(vmem_limit_bytes=VMEM),
        cost_estimate=pl.CostEstimate(
            flops=10**9, bytes_accessed=2**20, transcendentals=0
        ),
        name="slots",
    )(owner, lens, *groups, keys, values, part)


def merge_kernel(z1, z2, z3, owner_ref, pack_ref, late, *o_refs):
    count = o_refs[0].shape[0]
    for i, out in enumerate(o_refs):
        rows = slice((i + 1) * count, (i + 2) * count)
        parts = [opened(r[rows, :]) for r in (z1, z2, z3)]
        parts.append(local(late[i * count : (i + 1) * count, :]))
        put(out, *join(parts + [find_slots((i + 1) * count, count, owner_ref, pack_ref)]))


def home_kernel(z1, z2, z3, owner_ref, pack_ref, late, q_ref, nk_ref, nv_ref, out):
    count = out.shape[0]
    parts = [opened(r[:count, :]) for r in (z1, z2, z3)]
    parts += [local(late), own_part(q_ref, nk_ref, nv_ref)]
    put_local(out, *join(parts + [find_slots(0, count, owner_ref, pack_ref)]))


def merge(kernel, shapes, *args):
    return pl.pallas_call(
        kernel,
        out_shape=shapes,
        compiler_params=pltpu.CompilerParams(vmem_limit_bytes=VMEM),
        cost_estimate=pl.CostEstimate(flops=10**8, bytes_accessed=2**21, transcendentals=0),
        name="merge",
    )(*args)


def project_kernel(mine, x1, x2, x3, w_ref, keep_ref, send_ref, att):
    rows = mine.shape[0]
    att[...], _ = join([local(mine)] + [opened(r[...]) for r in (x1, x2, x3)])
    pre = lax.axis_index("pre")
    y = pre // 2
    core = pre % 2
    blocks = []
    for c in (core, 1 - core):
        for k in range(4):
            p = 2 * lax.rem(y + k, 4) + c
            blocks.append(att[pl.ds(pl.multiple_of(p * 8, 8), 8), :])
    ordered = jnp.concatenate(blocks, axis=0).astype(BF)
    out = jnp.dot(ordered, w_ref[...], preferred_element_type=F32)
    keep_ref[...] = out[: rows // 2]
    send_ref[...] = out[rows // 2 :].astype(BF)


def project(parts, w):
    rows = parts[0].shape[0]
    depth, width = w.shape
    return pl.pallas_call(
        project_kernel,
        out_shape=[
            jax.ShapeDtypeStruct((rows // 2, width), F32),
            jax.ShapeDtypeStruct((rows // 2, width), BF),
        ],
        scratch_shapes=[pltpu.VMEM((rows, 512), F32)],
        compiler_params=pltpu.CompilerParams(vmem_limit_bytes=VMEM),
        cost_estimate=pl.CostEstimate(flops=10**9, bytes_accessed=depth * width * 2, transcendentals=0),
        name="project",
    )(*parts, w)


def pair_kernel(keep_ref, got_ref, own_ref, s1, s2, s3):
    total = keep_ref[...] + got_ref[...].astype(F32)
    own_ref[...] = total[:8]
    for k, out in enumerate((s1, s2, s3)):
        out[...] = total[8 * (k + 1) : 8 * (k + 2)].astype(BF)


def pair(keep, got):
    width = keep.shape[1]
    return pl.pallas_call(
        pair_kernel,
        out_shape=[jax.ShapeDtypeStruct((8, width), F32)] + [jax.ShapeDtypeStruct((8, width), BF)] * 3,
        compiler_params=pltpu.CompilerParams(vmem_limit_bytes=VMEM),
        cost_estimate=pl.CostEstimate(flops=10**6, bytes_accessed=2**20, transcendentals=0),
        name="pair",
    )(keep, got)


def finish_kernel(own, r1, r2, r3, res, gain, o_ref):
    mixed = own[...] + r1[...].astype(F32) + r2[...].astype(F32) + r3[...].astype(F32)
    square = jnp.mean(mixed * mixed, axis=1, keepdims=True)
    o_ref[...] = (res[...].astype(F32) + gain[...] * mixed * lax.rsqrt(square + EPS)).astype(BF)


def finish(own, got, res, gain):
    return pl.pallas_call(
        finish_kernel,
        out_shape=jax.ShapeDtypeStruct(res.shape, BF),
        compiler_params=pltpu.CompilerParams(vmem_limit_bytes=56 * 2**20),
        cost_estimate=pl.CostEstimate(flops=10**6, bytes_accessed=2**19, transcendentals=0),
        name="finish",
    )(own, *got, res, gain)


def shift_x(a, k):
    return lax.ppermute(a, "rep", [(i, ((i // NZ + k) % 4) * NZ + i % NZ) for i in range(16)])


def shift_z(a, k):
    return lax.ppermute(a, "rep", [(i, (i // NZ) * NZ + (i % NZ + k) % NZ) for i in range(16)])


def shift_y(a, k):
    return lax.ppermute(a, "pre", [(i, ((i // 2 + k) % 4) * 2 + i % 2) for i in range(8)])


def swap_core(a):
    return lax.ppermute(a, "pre", [(i, i ^ 1) for i in range(8)])


def shards(
    residual_in,
    post_gain,
    queries,
    new_keys,
    new_values,
    prefix_keys,
    prefix_values,
    suffix_keys,
    suffix_values,
    suffix_len,
    slot_owner,
    output_weight,
):
    count = queries.shape[0]
    line = [queries] + [shift_x(queries, k) for k in (1, 2, 3)]
    owner = slot_owner[None, :]
    group0 = jnp.concatenate(line, axis=0)
    size = group0.shape[0]
    order = (1, 2, 3)
    rest = {k: shift_z(group0, k) for k in order}

    shifts = stage(group0, prefix_keys)
    shifts, rest[order[0]] = lax.optimization_barrier((shifts, rest[order[0]]))
    early = attend(plain_kernel, rest[order[0]], prefix_keys, prefix_values)
    groups = [group0, rest[1], rest[2], rest[3]]
    pack, part = slots(
        order[0], owner, suffix_len[None, :], groups, suffix_keys, suffix_values, early
    )
    back = [shift_z(part, -order[0])]
    for k in order[1:]:
        done = back[:-1]
        rest[k], part, *done = lax.optimization_barrier((rest[k], part, *done))
        back = done + back[-1:]
        part = attend(
            slotted_kernel, rest[k], prefix_keys, prefix_values, [owner, pack], k * size
        )
        back.append(shift_z(part, -k))
    group0, *done = lax.optimization_barrier((group0, *back[:-1]))
    back = done + back[-1:]
    wide = size - count
    late = attend(
        functools.partial(staged_kernel, count), group0, prefix_keys, prefix_values, [shifts], rows=wide
    )
    z = [*back, owner, pack]
    give = merge(merge_kernel, [jax.ShapeDtypeStruct((count, 640), BF)] * 3, *z, late)
    group0, *give = lax.optimization_barrier((group0, *give))
    far = shift_x(give[1], -2)
    x = [shift_x(give[0], -1), far, shift_x(give[2], -3)]
    near = attend(
        functools.partial(staged_kernel, 0), group0, prefix_keys, prefix_values, [shifts], rows=count
    )
    mine = merge(
        home_kernel,
        jax.ShapeDtypeStruct((count, 1024), F32),
        *z,
        near,
        queries,
        new_keys,
        new_values,
    )
    keep, send = project([mine, *x], output_weight)
    kept, *give = pair(keep, swap_core(send))
    far = shift_y(give[1], 2)
    got = [shift_y(give[0], 1), far, shift_y(give[2], 3)]
    return finish(kept, got, residual_in, post_gain[None, :])


def solution(mesh):
    return jax.shard_map(
        shards,
        mesh=mesh,
        in_specs=(
            P(("rep", "pre"), None),
            P(),
            P("rep", "pre"),
            P("rep", "pre"),
            P("rep", "pre"),
            P("rep", "pre"),
            P("rep", "pre"),
            P("rep", None, "pre"),
            P("rep", None, "pre"),
            P("rep"),
            P("rep"),
            P("pre", None),
        ),
        out_specs=P(("rep", "pre"), None),
        check_vma=False,
    )
```

```python
import functools
import math

import jax
import jax.numpy as jnp
from jax import lax
from jax.experimental import pallas as pl
from jax.experimental.pallas import tpu as pltpu
from jax.sharding import PartitionSpec as P

D = 4608
H = 32
HD = 128
EPS = 1e-06
NZ = 4
LOG2E = math.log2(math.e)
SCALE2 = (D // H) ** (-0.5) * LOG2E
LOW = -1e30
SAFE = 2.0**100
NT = (((1,), (1,)), ((), ()))
SAMPLE = 256
VMEM = 32 * 2**20
VMEM_ATT = 40 * 2**20
BF = jnp.bfloat16
F32 = jnp.float32


def pieces(x):
    hi = x.astype(BF)
    rest = x - hi.astype(F32)
    mid = rest.astype(BF)
    low = (rest - mid.astype(F32)).astype(BF)
    return hi, mid, low


def stat_tile(lse, rows):
    lane = lax.broadcasted_iota(jnp.int32, (rows, 128), 1)
    out = jnp.where(lane % 4 == 3, 1.0, 0.0)
    for h in range(4):
        for i, term in enumerate(pieces(lse[:, h * HD : (h + 1) * HD])):
            out = jnp.where(lane == 4 * h + i, term.astype(F32), out)
    return out.astype(BF)


def stat_spread(tile, flag=False):
    lane = lax.broadcasted_iota(jnp.int32, (128, 512), 0)
    head = lax.broadcasted_iota(jnp.int32, (128, 512), 1) // HD
    off = lane - 4 * head
    if flag:
        chosen = off == 3
    else:
        chosen = jnp.logical_and(off >= 0, off < 3)
    return jnp.dot(tile, jnp.where(chosen, 1.0, 0.0).astype(BF), preferred_element_type=F32)


def slot_rows(owner, count):
    bits = count.bit_length() - 1
    home = owner >> bits
    rep = lax.axis_index("rep")
    kx = (rep // NZ - (home >> 2)) & 3
    kz = (rep % NZ - (home & 3)) & 3
    return (kz << (bits + 2)) + (kx << bits) + (owner & (count - 1))


def find_slots(base, rows, owner_ref, pack_ref):
    where = slot_rows(owner_ref[...], pack_ref.shape[0])
    index = lax.broadcasted_iota(jnp.int32, (rows, where.shape[1]), 0) + base
    pick = jnp.where(index == where, 1.0, 0.0).astype(BF)
    found = jnp.dot(pick, pack_ref[...], preferred_element_type=F32)
    tile = found[:, 1024:].astype(BF)
    lse = jnp.where(stat_spread(tile, True) > 0.5, stat_spread(tile), LOW)
    return found[:, :512] + found[:, 512:1024], lse


def join(parts):
    both = functools.reduce(jnp.maximum, [x for _, x in parts])
    w = [jnp.exp2(x - both) for _, x in parts]
    mass = functools.reduce(jnp.add, w)
    o = functools.reduce(jnp.add, [v * x for (v, _), x in zip(parts, w)])
    return o / mass, both + jnp.log2(mass)


def opened(part):
    return part[:, :512].astype(F32), stat_spread(part[:, 512:])


def sampled(q_ref, k_ref, h):
    keys = k_ref[:SAMPLE, (h // 2) * HD : (h // 2 + 1) * HD]
    s = lax.dot_general(q_ref[:, h * HD : (h + 1) * HD], keys, NT, preferred_element_type=F32)
    return jnp.broadcast_to(jnp.max(s, axis=1, keepdims=True) * SCALE2, (q_ref.shape[0], 128))


def stage_kernel(q_ref, k_ref, o_ref):
    for h in range(4):
        o_ref[h] = sampled(q_ref, k_ref, h)


def stage(q, keys):
    rows = q.shape[0]
    return pl.pallas_call(
        stage_kernel,
        grid=(1,),
        in_specs=[
            pl.BlockSpec((rows, 512), lambda i: (0, 0)),
            pl.BlockSpec((SAMPLE, 256), lambda i: (0, 0)),
        ],
        out_specs=pl.BlockSpec((4, rows, 128), lambda i: (0, 0, 0)),
        out_shape=jax.ShapeDtypeStruct((4, rows, 128), F32),
        compiler_params=pltpu.CompilerParams(vmem_limit_bytes=VMEM),
        cost_estimate=pl.CostEstimate(flops=6 * 10**9, bytes_accessed=2**20, transcendentals=0),
        name="stage",
    )(q, keys)


def attend_body(q_ref, k_ref, v_ref, acc, top, first=None, start=0, loop=False):
    rows = acc.shape[1]
    span = k_ref.shape[0]
    mine = slice(start, start + rows)

    def lanes_of(n):
        return pl.ds(n * HD if isinstance(n, int) else pl.multiple_of(n * HD, HD), HD)

    def scores(heads, keys):
        q = [q_ref[mine, lanes_of(h)] for h in heads]
        q = jnp.concatenate(q, axis=0) if len(q) > 1 else q[0]
        return lax.dot_general(q, keys, NT, preferred_element_type=F32)

    for h in range(4):
        top[h] = sampled(q_ref, k_ref, h) if first is None else first[h, mine]

    def head_group(g, carry):
        values = jnp.concatenate([v_ref[:, lanes_of(g)], jnp.ones((span, 128), BF)], axis=1)
        keys = k_ref[:, lanes_of(g)]
        pair = [2 * g, 2 * g + 1]
        for heads in [pair] if rows < 128 else [pair[:1], pair[1:]]:
            shift = [top[h][:, :1] for h in heads]
            shift = jnp.concatenate(shift, axis=0) if len(shift) > 1 else shift[0]
            p = jnp.exp2(scores(heads, keys) * SCALE2 - shift).astype(BF)
            out = jnp.dot(p, values, preferred_element_type=F32)
            for n, h in enumerate(heads):
                acc[h] = out[n * rows : (n + 1) * rows]
        return carry

    if loop:
        lax.fori_loop(0, 2, head_group, 0)
    else:
        for g in range(2):
            head_group(g, 0)
    worst = jnp.zeros((rows, 128), F32)
    for h in range(4):
        worst = jnp.maximum(worst, jnp.where(acc[h][:, 128:] < SAFE, 0.0, 1.0))

    @pl.when(jnp.max(worst) > 0.0)
    def _():
        tile = math.gcd(span, 512)
        many = jnp.ones((tile, 128), BF)
        top[...] = jnp.full(top.shape, LOW, F32)
        acc[...] = jnp.zeros(acc.shape, F32)

        def tile_step(i, carry):
            h = i % 4
            part = pl.ds(pl.multiple_of((i // 4) * tile, tile), tile)
            values = jnp.concatenate([v_ref[part, lanes_of(h // 2)], many], axis=1)
            s = scores([h], k_ref[part, lanes_of(h // 2)]) * SCALE2
            old = top[h]
            new = jnp.maximum(old, jnp.max(s, axis=1, keepdims=True))
            p = jnp.exp2(s - new[:, :1]).astype(BF)
            fade = jnp.exp2(old - new)
            top[h] = new
            acc[h] = acc[h] * jnp.concatenate([fade, fade], axis=1) + jnp.dot(
                p, values, preferred_element_type=F32
            )
            return carry

        lax.fori_loop(0, 4 * (span // tile), tile_step, 0)

    totals = jnp.concatenate([acc[h][:, 128:] for h in range(4)], axis=1)
    o = jnp.concatenate([acc[h][:, :128] for h in range(4)], axis=1) / totals
    return o, jnp.concatenate([top[h] for h in range(4)], axis=1) + jnp.log2(totals)


def put(o_ref, o, lse):
    o_ref[:, :512] = o.astype(BF)
    o_ref[:, 512:] = stat_tile(lse, o_ref.shape[0])


def put_local(o_ref, o, lse):
    o_ref[:, :512] = o
    o_ref[:, 512:] = lse


def local(part):
    return part[:, :512], part[:, 512:]


def plain_kernel(q_ref, k_ref, v_ref, o_ref, acc, top):
    put_local(o_ref, *attend_body(q_ref, k_ref, v_ref, acc, top))


def staged_kernel(start, q_ref, k_ref, v_ref, first_ref, o_ref, acc, top):
    put_local(o_ref, *attend_body(q_ref, k_ref, v_ref, acc, top, first_ref, start))


def slotted_kernel(base, q_ref, k_ref, v_ref, owner_ref, pack_ref, o_ref, acc, top):
    part = attend_body(q_ref, k_ref, v_ref, acc, top, loop=True)
    put(o_ref, *join([part, find_slots(base[0], o_ref.shape[0], owner_ref, pack_ref)]))


def own_part(q_ref, nk_ref, nv_ref):
    score, value = [], []
    for h in range(4):
        lanes = slice((h // 2) * HD, (h // 2 + 1) * HD)
        prod = q_ref[:, h * HD : (h + 1) * HD].astype(F32) * nk_ref[:, lanes].astype(F32)
        total = jnp.sum(prod, axis=1, keepdims=True) * SCALE2
        score.append(jnp.broadcast_to(total, (q_ref.shape[0], HD)))
        value.append(nv_ref[:, lanes].astype(F32))
    return jnp.concatenate(value, axis=1), jnp.concatenate(score, axis=1)


def attend(kernel, q, keys, values, extra=(), base=None, rows=None):
    rows = rows or q.shape[0]
    span = keys.shape[0]
    vmem = pl.BlockSpec(memory_space=pltpu.VMEM)
    specs = [vmem] * (3 + len(extra))
    first = []
    if base is not None:
        specs = [pl.BlockSpec(memory_space=pltpu.SMEM)] + specs
        first = [jnp.full((1,), base, jnp.int32)]
    return pl.pallas_call(
        kernel,
        in_specs=specs,
        out_shape=jax.ShapeDtypeStruct(
            *(((rows, 1024), F32) if base is None else ((rows, 640), BF))
        ),
        scratch_shapes=[
            pltpu.VMEM((4, rows, 256), F32),
            pltpu.VMEM((4, rows, 128), F32),
        ],
        compiler_params=pltpu.CompilerParams(vmem_limit_bytes=VMEM_ATT),
        cost_estimate=pl.CostEstimate(
            flops=rows * 4 * span * 128, bytes_accessed=2**20, transcendentals=0
        ),
        name="attend",
    )(*first, q, keys, values, *extra)


def column(row):
    n = row.shape[1]
    same = lax.broadcasted_iota(jnp.int32, (n, n), 0) == lax.broadcasted_iota(jnp.int32, (n, n), 1)
    return jnp.sum(jnp.where(same, row.astype(F32), 0.0), axis=1, keepdims=True).astype(jnp.int32)


def slot_kernel(offset, owner_ref, lens_ref, g0, g1, g2, g3, k_ref, v_ref, part_ref, o_ref, merged_ref):
    count, depth, _ = k_ref.shape
    cols = count * depth
    size = g0.shape[0]
    where = column(slot_rows(owner_ref[...], count))
    q = jnp.zeros((count, 512), F32)
    for n, ref in enumerate((g0, g1, g2, g3)):
        index = lax.broadcasted_iota(jnp.int32, (count, size), 1) + n * size
        pick = jnp.where(index == where, 1.0, 0.0).astype(BF)
        q += jnp.dot(pick, ref[...], preferred_element_type=F32)
    q = q.astype(BF)
    off = lax.broadcasted_iota(jnp.int32, (count, cols), 1)
    off = off - depth * lax.broadcasted_iota(jnp.int32, (count, cols), 0)
    live = jnp.logical_and(off >= 0, off < column(lens_ref[...]))
    mask = jnp.where(live, 0.0, LOW)
    ones = jnp.ones((cols, 128), BF)
    lse = []
    for g in range(2):
        lanes = slice(g * HD, (g + 1) * HD)
        keys = k_ref[:, :, lanes].reshape(cols, HD)
        values = jnp.concatenate([v_ref[:, :, lanes].reshape(cols, HD), ones], axis=1)
        qq = [q[:, h * HD : (h + 1) * HD] for h in (2 * g, 2 * g + 1)]
        s = lax.dot_general(
            jnp.concatenate(qq, axis=0), keys, NT, preferred_element_type=F32
        )
        s = s * SCALE2 + jnp.concatenate([mask, mask], axis=0)
        m = jnp.max(s, axis=1, keepdims=True)
        acc = jnp.dot(jnp.exp2(s - m).astype(BF), values, preferred_element_type=F32)
        total = acc[:, 128:]
        both = acc[:, :128] / total
        log = m + jnp.log2(total)
        for j in range(2):
            h = 2 * g + j
            o = both[j * count : (j + 1) * count]
            hi = o.astype(BF)
            o_ref[:, h * HD : (h + 1) * HD] = hi
            o_ref[:, 512 + h * HD : 512 + (h + 1) * HD] = (o - hi.astype(F32)).astype(BF)
            lse.append(log[j * count : (j + 1) * count])
    o_ref[:, 1024:] = stat_tile(jnp.concatenate(lse, axis=1), count)
    found = find_slots(offset * size, part_ref.shape[0], owner_ref, o_ref)
    put(merged_ref, *join([local(part_ref), found]))


def slots(offset, owner, lens, groups, keys, values, part):
    count, depth, _ = keys.shape
    return pl.pallas_call(
        functools.partial(slot_kernel, offset),
        out_shape=[
            jax.ShapeDtypeStruct((count, 1152), BF),
            jax.ShapeDtypeStruct((part.shape[0], 640), BF),
        ],
        compiler_params=pltpu.CompilerParams(vmem_limit_bytes=VMEM),
        cost_estimate=pl.CostEstimate(
            flops=10**9, bytes_accessed=2**20, transcendentals=0
        ),
        name="slots",
    )(owner, lens, *groups, keys, values, part)


def merge_kernel(z1, z2, z3, owner_ref, pack_ref, late, *o_refs):
    count = o_refs[0].shape[0]
    for i, out in enumerate(o_refs):
        rows = slice((i + 1) * count, (i + 2) * count)
        parts = [opened(r[rows, :]) for r in (z1, z2, z3)]
        parts.append(local(late[i * count : (i + 1) * count, :]))
        put(out, *join(parts + [find_slots((i + 1) * count, count, owner_ref, pack_ref)]))


def home_kernel(z1, z2, z3, owner_ref, pack_ref, late, q_ref, nk_ref, nv_ref, out):
    count = out.shape[0]
    parts = [opened(r[:count, :]) for r in (z1, z2, z3)]
    parts += [local(late), own_part(q_ref, nk_ref, nv_ref)]
    put_local(out, *join(parts + [find_slots(0, count, owner_ref, pack_ref)]))


def merge(kernel, shapes, *args):
    return pl.pallas_call(
        kernel,
        out_shape=shapes,
        compiler_params=pltpu.CompilerParams(vmem_limit_bytes=VMEM),
        cost_estimate=pl.CostEstimate(flops=10**8, bytes_accessed=2**21, transcendentals=0),
        name="merge",
    )(*args)


def project_kernel(mine, x1, x2, x3, w_ref, keep_ref, send_ref, att):
    rows = mine.shape[0]
    att[...], _ = join([local(mine)] + [opened(r[...]) for r in (x1, x2, x3)])
    pre = lax.axis_index("pre")
    y = pre // 2
    core = pre % 2
    blocks = []
    for c in (core, 1 - core):
        for k in range(4):
            p = 2 * lax.rem(y + k, 4) + c
            blocks.append(att[pl.ds(pl.multiple_of(p * 8, 8), 8), :])
    ordered = jnp.concatenate(blocks, axis=0).astype(BF)
    out = jnp.dot(ordered, w_ref[...], preferred_element_type=F32)
    keep_ref[...] = out[: rows // 2]
    send_ref[...] = out[rows // 2 :].astype(BF)


def project(parts, w):
    rows = parts[0].shape[0]
    depth, width = w.shape
    return pl.pallas_call(
        project_kernel,
        out_shape=[
            jax.ShapeDtypeStruct((rows // 2, width), F32),
            jax.ShapeDtypeStruct((rows // 2, width), BF),
        ],
        scratch_shapes=[pltpu.VMEM((rows, 512), F32)],
        compiler_params=pltpu.CompilerParams(vmem_limit_bytes=VMEM),
        cost_estimate=pl.CostEstimate(flops=10**9, bytes_accessed=depth * width * 2, transcendentals=0),
        name="project",
    )(*parts, w)


def pair_kernel(keep_ref, got_ref, own_ref, s1, s2, s3):
    total = keep_ref[...] + got_ref[...].astype(F32)
    own_ref[...] = total[:8]
    for k, out in enumerate((s1, s2, s3)):
        out[...] = total[8 * (k + 1) : 8 * (k + 2)].astype(BF)


def pair(keep, got):
    width = keep.shape[1]
    return pl.pallas_call(
        pair_kernel,
        out_shape=[jax.ShapeDtypeStruct((8, width), F32)] + [jax.ShapeDtypeStruct((8, width), BF)] * 3,
        compiler_params=pltpu.CompilerParams(vmem_limit_bytes=VMEM),
        cost_estimate=pl.CostEstimate(flops=10**6, bytes_accessed=2**20, transcendentals=0),
        name="pair",
    )(keep, got)


def finish_kernel(own, r1, r2, r3, res, gain, o_ref):
    mixed = own[...] + r1[...].astype(F32) + r2[...].astype(F32) + r3[...].astype(F32)
    square = jnp.mean(mixed * mixed, axis=1, keepdims=True)
    o_ref[...] = (res[...].astype(F32) + gain[...] * mixed * lax.rsqrt(square + EPS)).astype(BF)


def finish(own, got, res, gain):
    return pl.pallas_call(
        finish_kernel,
        out_shape=jax.ShapeDtypeStruct(res.shape, BF),
        compiler_params=pltpu.CompilerParams(vmem_limit_bytes=VMEM),
        cost_estimate=pl.CostEstimate(flops=10**6, bytes_accessed=2**19, transcendentals=0),
        name="finish",
    )(own, *got, res, gain)


def shift_x(a, k):
    return lax.ppermute(a, "rep", [(i, ((i // NZ + k) % 4) * NZ + i % NZ) for i in range(16)])


def shift_z(a, k):
    return lax.ppermute(a, "rep", [(i, (i // NZ) * NZ + (i % NZ + k) % NZ) for i in range(16)])


def shift_y(a, k):
    return lax.ppermute(a, "pre", [(i, ((i // 2 + k) % 4) * 2 + i % 2) for i in range(8)])


def swap_core(a):
    return lax.ppermute(a, "pre", [(i, i ^ 1) for i in range(8)])


def shards(
    residual_in,
    post_gain,
    queries,
    new_keys,
    new_values,
    prefix_keys,
    prefix_values,
    suffix_keys,
    suffix_values,
    suffix_len,
    slot_owner,
    output_weight,
):
    count = queries.shape[0]
    line = [queries] + [shift_x(queries, k) for k in (1, 2, 3)]
    owner = slot_owner[None, :]
    group0 = jnp.concatenate(line, axis=0)
    size = group0.shape[0]
    order = (1, 2, 3)
    rest = {k: shift_z(group0, k) for k in order}

    shifts = stage(group0, prefix_keys[:SAMPLE])
    shifts, rest[order[0]] = lax.optimization_barrier((shifts, rest[order[0]]))
    early = attend(plain_kernel, rest[order[0]], prefix_keys, prefix_values)
    groups = [group0, rest[1], rest[2], rest[3]]
    pack, part = slots(
        order[0], owner, suffix_len[None, :], groups, suffix_keys, suffix_values, early
    )
    back = [shift_z(part, -order[0])]
    for k in order[1:]:
        done = back[:-1]
        rest[k], part, *done = lax.optimization_barrier((rest[k], part, *done))
        back = done + back[-1:]
        part = attend(
            slotted_kernel, rest[k], prefix_keys, prefix_values, [owner, pack], k * size
        )
        back.append(shift_z(part, -k))
    group0, *done = lax.optimization_barrier((group0, *back[:-1]))
    back = done + back[-1:]
    wide = size - count
    late = attend(
        functools.partial(staged_kernel, count), group0, prefix_keys, prefix_values, [shifts], rows=wide
    )
    z = [*back, owner, pack]
    give = merge(merge_kernel, [jax.ShapeDtypeStruct((count, 640), BF)] * 3, *z, late)
    group0, *give = lax.optimization_barrier((group0, *give))
    x = [shift_x(a, -k) for k, a in zip((1, 2, 3), give)]
    near = attend(
        functools.partial(staged_kernel, 0), group0, prefix_keys, prefix_values, [shifts], rows=count
    )
    mine = merge(
        home_kernel,
        jax.ShapeDtypeStruct((count, 1024), F32),
        *z,
        near,
        queries,
        new_keys,
        new_values,
    )
    keep, send = project([mine, *x], output_weight)
    kept, *give = pair(keep, swap_core(send))
    got = [shift_y(a, k) for k, a in zip((1, 2, 3), give)]
    return finish(kept, got, residual_in, post_gain[None, :])


def solution(mesh):
    return jax.shard_map(
        shards,
        mesh=mesh,
        in_specs=(
            P(("rep", "pre"), None),
            P(),
            P("rep", "pre"),
            P("rep", "pre"),
            P("rep", "pre"),
            P("rep", "pre"),
            P("rep", "pre"),
            P("rep", None, "pre"),
            P("rep", None, "pre"),
            P("rep"),
            P("rep"),
            P("pre", None),
        ),
        out_specs=P(("rep", "pre"), None),
        check_vma=False,
    )
```
